256 devices in a mesh: pts: 128 (over y, z_lo, x, core), lab: 2 (over z_hi).
Axes of the slice: x: 4, y: 4, z: 8 (z_hi: 2, z_lo: 4; z = z_hi * 4 + z_lo), core: 2. Of those that a mesh axis runs over, the one named last changes fastest.
Arguments:
- slab_points: bfloat16 [8192, 128], P('pts'), may hold values from -6 to 6
- key_points: bfloat16 [131072, 128], P('pts'), may hold values from -6 to 6
- length_weights: float32 [128], replicated, may hold values from 0.5 to 2
- adjoint: bfloat16 [131072, 256], P('pts', 'lab'), may hold values from -0.875 to 0.875
- label_cov: float32 [256, 256], P('lab'), may hold values from -0.375 to 0.375
- cotangent: bfloat16 [8192, 256], P('pts', 'lab'), may hold values from -0.0625 to 0.0625
Outputs:
- mixed_rows: bfloat16 [8192, 256], P('pts', 'lab')
- cov_grad: float32 [256, 256], P('lab')
The draws below stay inside these ranges and needn't reach their ends.
All inputs are finite; a program needn't handle non-finite values.
Results may differ from the reference program's by a relative error of at most 0.005.
Values may be sent and summed in bfloat16 or wider, within the bound.
No kernel may reach another device: no remote copies, remote signals or barrier semaphores. Data moves between devices by JAX's collectives and lax.ppermute only.
A program may use at most 64 MiB of HBM per device.

```python
import math
import jax
import jax.numpy as jnp
from jax import lax

F = 128
L = 256
KEY_DEV = 1024
NKEYS = 131072
SLAB = 8192


def block_levels(rng, dims, split, least, largest):
    loudness = 1.0
    for dim, parts in split:
        heights = jax.random.uniform(jax.random.fold_in(jax.random.fold_in(rng, 6), dim), (parts,), jnp.float32, least / len(split), largest / len(split))
        loudness = loudness * jnp.repeat(jnp.exp(heights), dims[dim] // parts).reshape((-1,) + (1,) * (len(dims) - 1 - dim))
    return loudness


def gaussian(own_key, dims, deviation, reach, cuts=(), kind=jnp.bfloat16):
    loudness = block_levels(own_key, dims, cuts, -0.22, 0.18) if cuts else 1.0
    result = jax.random.normal(own_key, dims, jnp.float32) * deviation * loudness
    return jnp.minimum(jnp.maximum(result, -reach), reach).astype(kind)


def setup_inputs(seed: int = 0) -> dict:
    streams_of = jax.random.split(jax.random.key(seed), 7)
    slab_points = gaussian(streams_of[0], (SLAB, F), 1.0, 6.0, ((0, 128),))
    key_points = gaussian(streams_of[1], (NKEYS, F), 1.0, 6.0, ((0, 128),))
    length_weights = jnp.clip(jnp.exp(jax.random.uniform(streams_of[2], (F,), jnp.float32, math.log(0.5), math.log(2.0))), 0.5, 2.0)
    adjoint = gaussian(streams_of[3], (NKEYS, L), (50.0 / NKEYS ** 0.5), 0.875, ((0, 128), (1, 2)))
    label_cov = gaussian(streams_of[4], (L, L), L ** -0.5, 0.375, ((0, 2),), jnp.float32)
    cotangent = gaussian(streams_of[5], (SLAB, L), (1.0 / SLAB ** 0.5), 0.0625, ((0, 128), (1, 2)))
    return {"slab_points": slab_points, "key_points": key_points, "length_weights": length_weights, "adjoint": adjoint, "label_cov": label_cov, "cotangent": cotangent}


def sq_norms(rows, weights):
    wide = rows.astype(jnp.float32)
    return jnp.sum(wide * wide * weights, axis=1)


def kernel_tile(slab_rows, slab_sq, scaled_keys, key_sq, width):
    inner = lax.dot_general(slab_rows, scaled_keys, (((1,), (1,)), ((), ())), preferred_element_type=jnp.float32)
    dist = slab_sq[:, None] + key_sq[None, :] - 2.0 * inner
    return jnp.exp(dist * (-2.0 / width)).astype(jnp.bfloat16)


def reference(slab_points, key_points, length_weights, adjoint, label_cov, cotangent):
    width = slab_points.shape[1]
    slab_sq = sq_norms(slab_points, length_weights)
    scaled = (key_points.astype(jnp.float32) * length_weights).astype(jnp.bfloat16)
    key_sq = sq_norms(key_points, length_weights)
    blocks = key_points.shape[0] // KEY_DEV

    def step(total, index):
        start = (index * KEY_DEV).astype(jnp.int32)
        keys_block = lax.dynamic_slice_in_dim(scaled, start, KEY_DEV, 0)
        sq_block = lax.dynamic_slice_in_dim(key_sq, start, KEY_DEV, 0)
        adj_block = lax.dynamic_slice_in_dim(adjoint, start, KEY_DEV, 0)
        tile = kernel_tile(slab_points, slab_sq, keys_block, sq_block, width)
        return total + jnp.dot(tile, adj_block, preferred_element_type=jnp.float32), None

    start_total = jnp.zeros((slab_points.shape[0], adjoint.shape[1]), jnp.float32)
    cross, _ = lax.scan(step, start_total, jnp.arange(blocks, dtype=jnp.int32))
    mixed = jnp.dot(cross, label_cov, precision=lax.Precision.HIGHEST, preferred_element_type=jnp.float32).astype(jnp.bfloat16)
    grad = jnp.dot(cross.T, cotangent.astype(jnp.float32), precision=lax.Precision.HIGHEST, preferred_element_type=jnp.float32)
    return mixed, grad
```

```python
import jax
import jax.numpy as jnp
from jax import lax
from jax.experimental import pallas as pl
from jax.experimental.pallas import tpu as pltpu
from jax.sharding import PartitionSpec as P

F32 = jnp.float32
BF16 = jnp.bfloat16
PTS = 128
KEYS = 1024
TILE = 256
CORE, X, Z, Y = 0, 1, 3, 5


def swap(value, place, mask):
    return lax.ppermute(value, "pts", [(i, i ^ (mask << place)) for i in range(PTS)])


def swap_lab(value):
    return lax.ppermute(value, "lab", [(0, 1), (1, 0)])


def cross_kernel(weights_ref, rows_ref, *refs):
    packs, wide_ref, sent_ref = refs[:-2], refs[-2], refs[-1]
    rows = rows_ref[:, 0:128]
    wide = rows.astype(F32)
    row_term = jnp.sum(wide * wide * weights_ref[...], axis=1, keepdims=True) * (-1.0 / 64.0)
    total = jnp.zeros((rows.shape[0], 128), F32)
    for pack in packs:
        parts = pack[KEYS : KEYS + 16, :].astype(F32)
        for j in range(KEYS // TILE):
            key_term = parts[j : j + 1] + parts[4 + j : 5 + j] + parts[8 + j : 9 + j]
            tile = pl.ds(j * TILE, TILE)
            inner = lax.dot_general(
                rows, pack[tile, 0:128], (((1,), (1,)), ((), ())), preferred_element_type=F32
            )
            kernel = jnp.exp(inner + row_term + key_term).astype(BF16)
            total += jnp.dot(kernel, pack[tile, 128:256], preferred_element_type=F32)
    wide_ref[...] = total
    sent_ref[...] = total.astype(BF16)


def cross_block(weights, rows, packs):
    count = rows.shape[0]
    return pl.pallas_call(
        cross_kernel,
        out_shape=(
            jax.ShapeDtypeStruct((count, 128), F32),
            jax.ShapeDtypeStruct((count, 128), BF16),
        ),
        in_specs=[pl.BlockSpec(memory_space=pltpu.VMEM)] * (2 + len(packs)),
        out_specs=(pl.BlockSpec(memory_space=pltpu.VMEM),) * 2,
        compiler_params=pltpu.CompilerParams(vmem_limit_bytes=40 * 2**20),
        cost_estimate=pl.CostEstimate(
            flops=4 * count * len(packs) * KEYS * 128,
            bytes_accessed=5 * 2**20,
            transcendentals=count * len(packs) * KEYS,
        ),
        name="cross_block",
    )(weights, rows, *packs)


def local(slab_points, key_points, length_weights, adjoint, label_cov, cotangent):
    first_core = lax.axis_index("pts") % 2 == 0
    first_lab = lax.axis_index("lab") == 0

    keys = key_points.astype(F32)
    scaled = (keys * length_weights * (1.0 / 32.0)).astype(BF16)
    key_term = jnp.sum(keys * keys * length_weights, axis=1) * (-1.0 / 64.0)
    high = lax.reduce_precision(key_term, 8, 7)
    rest = key_term - high
    middle = lax.reduce_precision(rest, 8, 7)
    parts = jnp.stack([high, middle, rest - middle, jnp.zeros_like(high)]).reshape(16, 256)
    pack = jnp.concatenate(
        [jnp.concatenate([scaled, adjoint], axis=1), parts.astype(BF16)], axis=0
    )
    packs = [pack] + [swap(pack, X, m) for m in (1, 2, 3)]
    packs = packs + [swap(p, CORE, 1) for p in packs]

    own = jnp.concatenate([slab_points, cotangent], axis=1)
    over_z = jnp.concatenate([own] + [swap(own, Z, m) for m in (1, 2, 3)], axis=0)
    rows = [over_z] + [swap(over_z, Y, m) for m in (1, 2, 3)]
    cot = jnp.concatenate([r[:, 128:] for r in rows], axis=0)
    cot_far = swap_lab(cot)

    weights = length_weights.reshape(1, 128)
    blocks = {m: cross_block(weights, rows[m], packs) for m in (2, 1, 3, 0)}
    back = {m: swap(blocks[m][1], Y, m).astype(F32) for m in (2, 1, 3)}
    over_y = (blocks[0][0] + back[1]) + (back[2] + back[3])

    sent = jnp.concatenate([blocks[m][1] for m in range(4)], axis=0)
    turned = (((0,), (0,)), ((), ()))
    grad = jnp.concatenate(
        [lax.dot_general(sent, c, turned, preferred_element_type=F32) for c in (cot, cot_far)],
        axis=1,
    )
    upper, lower = grad[:64], grad[64:]
    grad = jnp.where(first_core, upper, lower) + swap(
        jnp.where(first_core, lower, upper), CORE, 1
    )

    joint = [jnp.concatenate([over_y[64 * m : 64 * m + 64], grad], axis=1) for m in range(4)]
    back = [swap(joint[m], Z, m) for m in (1, 2, 3)]
    joint = (joint[0] + back[0]) + (back[1] + back[2])
    cross, grad = joint[:, :128], joint[:, 128:]

    back = [swap(grad, Y, m) for m in (1, 2, 3)]
    part = jnp.dot(cross, label_cov, precision=lax.Precision.HIGHEST, preferred_element_type=F32)
    near, far = part[:, :128], part[:, 128:]
    mixed = jnp.where(first_lab, near, far) + swap_lab(jnp.where(first_lab, far, near))

    grad = (grad + back[0]) + (back[1] + back[2])
    back = [swap(grad, X, m) for m in (1, 2, 3)]
    grad = (grad + back[0]) + (back[1] + back[2])
    grad = jnp.where(
        first_lab, grad, jnp.concatenate([grad[:, 128:], grad[:, :128]], axis=1)
    )
    other = swap(grad, CORE, 1)
    grad = jnp.where(
        first_core,
        jnp.concatenate([grad, other], axis=0),
        jnp.concatenate([other, grad], axis=0),
    )
    return mixed.astype(BF16), grad


def solution(mesh):
    placed = (P("pts", None), P("pts", None), P(), P("pts", "lab"), P("lab", None), P("pts", "lab"))
    return jax.shard_map(
        local,
        mesh=mesh,
        in_specs=placed,
        out_specs=(P("pts", "lab"), P("lab", None)),
        check_vma=False,
    )
```

```python
import functools

import jax
import jax.numpy as jnp
from jax import lax
from jax.experimental import pallas as pl
from jax.experimental.pallas import tpu as pltpu
from jax.sharding import PartitionSpec as P

F32 = jnp.float32
BF16 = jnp.bfloat16
PTS = 128
HALF = 512
TILE = 256
CORE, X, Z, Y = 0, 1, 3, 5


def swap(value, place, mask):
    return lax.ppermute(value, "pts", [(i, i ^ (mask << place)) for i in range(PTS)])


def swap_ring(value, place, step):
    pairs = []
    for i in range(PTS):
        at = (i >> place) & 3
        pairs.append((i, i + ((((at - step) & 3) - at) << place)))
    return lax.ppermute(value, "pts", pairs)


def swap_lab(value):
    return lax.ppermute(value, "lab", [(0, 1), (1, 0)])


def after(value, *earlier):
    return lax.optimization_barrier((value, *earlier))[0]


def accumulate(total, rows, row_term, pack):
    for base in range(0, pack.shape[0], HALF + 16):
        terms = pack[base + HALF : base + HALF + 16, :].astype(F32)
        for j in range(HALF // TILE):
            key_term = terms[j : j + 1] + terms[4 + j : 5 + j] + terms[8 + j : 9 + j]
            tile = pl.ds(base + j * TILE, TILE)
            inner = lax.dot_general(
                rows, pack[tile, 0:128], (((1,), (1,)), ((), ())), preferred_element_type=F32
            )
            kernel = jnp.exp(inner + row_term + key_term).astype(BF16)
            total += jnp.dot(kernel, pack[tile, 128:256], preferred_element_type=F32)
    return total


def term_of(weights_ref, rows):
    wide = rows.astype(F32)
    return jnp.sum(wide * wide * weights_ref[...], axis=1, keepdims=True) * (-1.0 / 64.0)


def first_kernel(has_total, weights_ref, *refs):
    row_refs, refs = refs[:4], refs[4:]
    start, refs = (refs[0], refs[1:]) if has_total else (None, refs)
    packs, out = refs[:-1], refs[-1]
    for m, row_ref in enumerate(row_refs):
        rows = row_ref[:, 0:128]
        row_term = term_of(weights_ref, rows)
        total = start[256 * m : 256 * m + 256, :] if has_total else jnp.zeros((256, 128), F32)
        for pack in packs:
            total = accumulate(total, rows, row_term, pack)
        out[256 * m : 256 * m + 256, :] = total


def last_kernel(m, weights_ref, row_ref, start, *refs):
    packs, out = refs[:-1], refs[-1]
    rows = row_ref[:, 0:128]
    total = start[256 * m : 256 * m + 256, :]
    row_term = term_of(weights_ref, rows)
    for pack in packs:
        total = accumulate(total, rows, row_term, pack)
    out[...] = total.astype(out.dtype)


def in_vmem(kernel, out, args, keys):
    rows = out.shape[0]
    return pl.pallas_call(
        kernel,
        out_shape=out,
        in_specs=[pl.BlockSpec(memory_space=pltpu.VMEM)] * len(args),
        out_specs=pl.BlockSpec(memory_space=pltpu.VMEM),
        compiler_params=pltpu.CompilerParams(vmem_limit_bytes=16 * 2**20),
        cost_estimate=pl.CostEstimate(
            flops=4 * rows * keys * 128,
            bytes_accessed=2**20,
            transcendentals=rows * keys,
        ),
    )(*args)


def cross_first(weights, rows, total, packs):
    has_total = total is not None
    args = [weights, *rows] + ([total] if has_total else []) + list(packs)
    return in_vmem(
        functools.partial(first_kernel, has_total),
        jax.ShapeDtypeStruct((1024, 128), F32),
        args,
        sum(p.shape[0] for p in packs),
    )


def cross_last(m, weights, rows, total, packs, dtype):
    return in_vmem(
        functools.partial(last_kernel, m),
        jax.ShapeDtypeStruct((256, 128), dtype),
        [weights, rows, total, *packs],
        sum(p.shape[0] for p in packs),
    )


def grad_kernel(*refs):
    sent, rows, far, out = refs[:4], refs[4:8], refs[8], refs[9]
    turned = (((0,), (0,)), ((), ()))
    near_sum = jnp.zeros((128, 128), F32)
    far_sum = jnp.zeros((128, 128), F32)
    for m in range(4):
        left = sent[m][...].astype(BF16)
        near_sum += lax.dot_general(left, rows[m][:, 128:256], turned, preferred_element_type=F32)
        far_sum += lax.dot_general(
            left, far[256 * m : 256 * m + 256, :], turned, preferred_element_type=F32
        )
    out[:, 0:128] = near_sum
    out[:, 128:256] = far_sum


def local(slab_points, key_points, length_weights, adjoint, label_cov, cotangent):
    first_core = lax.axis_index("pts") % 2 == 0
    first_lab = lax.axis_index("lab") == 0
    weights = length_weights.reshape(1, 128)

    keys = key_points.astype(F32)
    scaled = (keys * length_weights * (1.0 / 32.0)).astype(BF16)
    key_term = jnp.sum(keys * keys * length_weights, axis=1) * (-1.0 / 64.0)
    high = lax.reduce_precision(key_term, 8, 7)
    rest = key_term - high
    middle = lax.reduce_precision(rest, 8, 7)
    both = jnp.concatenate([scaled, adjoint], axis=1)
    halves = []
    for h in (slice(0, HALF), slice(HALF, 2 * HALF)):
        blank = jnp.zeros((2, 256), F32)
        parts = [jnp.concatenate([t[h].reshape(2, 256), blank]) for t in (high, middle, rest - middle)]
        parts = jnp.concatenate([*parts, blank, blank]).astype(BF16)
        halves += [both[h], parts]
    pack = jnp.concatenate(halves, axis=0)

    right = swap_ring(pack, X, 1)
    left = swap_ring(pack, X, 3)
    own_far = swap(pack, CORE, 1)

    own = jnp.concatenate([slab_points, cotangent], axis=1)
    over_z = jnp.concatenate([own] + [swap(own, Z, m) for m in (1, 2, 3)], axis=0)
    rows = [over_z] + [swap(over_z, Y, m) for m in (1, 2, 3)]

    right, left = after(right, *rows), after(left, *rows)
    upper = swap_ring(right[:528], X, 1)
    lower = swap_ring(left[528:], X, 3)
    right_far, left_far = swap(right, CORE, 1), swap(left, CORE, 1)
    cot = jnp.concatenate([r[:, 128:] for r in rows], axis=0)
    cot_far = swap_lab(cot)

    total = cross_first(weights, rows, None, [pack, own_far, right, right_far])
    upper, lower = after(upper, total), after(lower, total)
    upper_far, lower_far = swap(upper, CORE, 1), swap(lower, CORE, 1)
    total = cross_first(weights, rows, total, [left, left_far])
    packs = [upper, lower, upper_far, lower_far]
    sent = {
        m: cross_last(m, weights, rows[m], total, packs, F32 if m == 0 else BF16)
        for m in (2, 1, 3, 0)
    }
    back = {m: swap(sent[m], Y, m).astype(F32) for m in (2, 1, 3)}
    over_y = (sent[0] + back[1]) + (back[2] + back[3])

    grad = in_vmem(
        grad_kernel,
        jax.ShapeDtypeStruct((128, 256), F32),
        [sent[m] for m in range(4)] + rows + [cot_far],
        256,
    )
    upper, lower = grad[:64], grad[64:]
    grad = jnp.where(first_core, upper, lower) + swap(
        jnp.where(first_core, lower, upper), CORE, 1
    )

    joint = [jnp.concatenate([over_y[64 * m : 64 * m + 64], grad], axis=1) for m in range(4)]
    back = [swap(joint[m], Z, m) for m in (1, 2, 3)]
    joint = (joint[0] + back[0]) + (back[1] + back[2])
    cross, grad = joint[:, :128], joint[:, 128:]

    back = [swap(grad, Y, m) for m in (1, 2, 3)]
    part = jnp.dot(cross, label_cov, precision=lax.Precision.HIGHEST, preferred_element_type=F32)
    near, far = part[:, :128], part[:, 128:]
    mixed = jnp.where(first_lab, near, far) + swap_lab(jnp.where(first_lab, far, near))

    grad = (grad + back[0]) + (back[1] + back[2])
    back = [swap(grad, X, m) for m in (1, 2, 3)]
    grad = (grad + back[0]) + (back[1] + back[2])
    grad = jnp.where(
        first_lab, grad, jnp.concatenate([grad[:, 128:], grad[:, :128]], axis=1)
    )
    other = swap(grad, CORE, 1)
    grad = jnp.where(
        first_core,
        jnp.concatenate([grad, other], axis=0),
        jnp.concatenate([other, grad], axis=0),
    )
    return mixed.astype(BF16), grad


def solution(mesh):
    placed = (P("pts", None), P("pts", None), P(), P("pts", "lab"), P("lab", None), P("pts", "lab"))
    return jax.shard_map(
        local,
        mesh=mesh,
        in_specs=placed,
        out_specs=(P("pts", "lab"), P("lab", None)),
        check_vma=False,
    )
```

```python
import functools

import jax
import jax.numpy as jnp
from jax import lax
from jax.experimental import pallas as pl
from jax.experimental.pallas import tpu as pltpu
from jax.sharding import PartitionSpec as P

F32 = jnp.float32
BF16 = jnp.bfloat16
PTS = 128
HALF = 512
TILE = 256
CORE, X, Z, Y = 0, 1, 3, 5


def swap(value, place, mask):
    return lax.ppermute(value, "pts", [(i, i ^ (mask << place)) for i in range(PTS)])


def swap_ring(value, place, step):
    pairs = []
    for i in range(PTS):
        at = (i >> place) & 3
        pairs.append((i, i + ((((at - step) & 3) - at) << place)))
    return lax.ppermute(value, "pts", pairs)


def swap_lab(value):
    return lax.ppermute(value, "lab", [(0, 1), (1, 0)])


def accumulate(total, rows, row_term, pack):
    for base in range(0, pack.shape[0], HALF + 16):
        terms = pack[base + HALF : base + HALF + 16, :].astype(F32)
        for j in range(HALF // TILE):
            key_term = terms[j : j + 1] + terms[4 + j : 5 + j] + terms[8 + j : 9 + j]
            tile = pl.ds(base + j * TILE, TILE)
            inner = lax.dot_general(
                rows, pack[tile, 0:128], (((1,), (1,)), ((), ())), preferred_element_type=F32
            )
            kernel = jnp.exp(inner + row_term + key_term).astype(BF16)
            total += jnp.dot(kernel, pack[tile, 128:256], preferred_element_type=F32)
    return total


def prepare_kernel(weights_ref, *refs):
    part_refs, (rows_ref, term_ref, cot_ref, zero_ref) = refs[:4], refs[4:]
    weights = weights_ref[...].reshape(1, 128) * (-1.0 / 64.0)
    for d, ref in enumerate(part_refs):
        for m in range(4):
            place = pl.ds(256 * m + 64 * d, 64)
            part = ref[64 * m : 64 * m + 64, :]
            wide = part.astype(F32)
            rows_ref[place, :] = part
            term = jnp.sum(wide * wide * weights, axis=1, keepdims=True)
            term_ref[place, :] = jnp.broadcast_to(term, (64, 128))
        cot_ref[64 * d : 64 * d + 64, :] = ref[256:320, :]
    zero_ref[...] = jnp.zeros_like(zero_ref)


def first_kernel(has_total, *refs):
    rows_ref, term_ref, refs = refs[0], refs[1], refs[2:]
    start, refs = (refs[0], refs[1:]) if has_total else (None, refs)
    packs, out, zero_ref = refs[:-2], refs[-2], refs[-1]
    for m in range(4):
        place = slice(256 * m, 256 * m + 256)
        total = start[place, :] if has_total else jnp.zeros((256, 128), F32)
        for pack in packs:
            total = accumulate(total, rows_ref[place, :], term_ref[place, 0:1], pack)
        out[place, :] = total
    zero_ref[...] = jnp.zeros_like(zero_ref)


def last_kernel(m, *refs):
    rows_ref, term_ref, start, packs, out = refs[0], refs[1], refs[2], refs[3:-1], refs[-1]
    place = slice(256 * m, 256 * m + 256)
    total = start[place, :]
    for pack in packs:
        total = accumulate(total, rows_ref[place, :], term_ref[place, 0:1], pack)
    out[...] = total.astype(out.dtype)


def in_vmem(kernel, out, args, small=None, scratch=()):
    spaces = [pltpu.VMEM] * len(args)
    if small is not None:
        spaces[small] = pltpu.SMEM
    return pl.pallas_call(
        kernel,
        out_shape=out,
        in_specs=[pl.BlockSpec(memory_space=space) for space in spaces],
        scratch_shapes=scratch,
        out_specs=jax.tree.map(lambda _: pl.BlockSpec(memory_space=pltpu.VMEM), out),
        compiler_params=pltpu.CompilerParams(vmem_limit_bytes=8 * 2**20),
        cost_estimate=pl.CostEstimate(
            flops=1000,
            bytes_accessed=2 * 2**20,
            transcendentals=0,
        ),
    )(*args)


ZEROS = jax.ShapeDtypeStruct((16, 256), BF16)


def prepare(weights, rows):
    return in_vmem(
        prepare_kernel,
        (
            jax.ShapeDtypeStruct((1024, 128), BF16),
            jax.ShapeDtypeStruct((1024, 128), F32),
            jax.ShapeDtypeStruct((256, 128), BF16),
            ZEROS,
        ),
        [weights, *rows],
    )


def cross_first(rows, term, total, packs):
    has_total = total is not None
    return in_vmem(
        functools.partial(first_kernel, has_total),
        (jax.ShapeDtypeStruct((1024, 128), F32), ZEROS),
        [rows, term] + ([total] if has_total else []) + list(packs),
    )


def cross_last(m, rows, term, total, packs, dtype):
    return in_vmem(
        functools.partial(last_kernel, m),
        jax.ShapeDtypeStruct((256, 128), dtype),
        [rows, term, total, *packs],
    )


def gate_kernel(value_ref, _, out_ref):
    out_ref[...] = value_ref[...]


def grad_kernel(place_ref, own, *refs):
    back, near, far, cov_ref = refs[:3], refs[3], refs[4], refs[5]
    mixed_ref, mixed_far_ref, grad_ref, grad_far_ref, held = refs[6:]
    own_columns = pl.ds(pl.multiple_of(place_ref[0] * 128, 128), 128)
    far_columns = pl.ds(pl.multiple_of(128 - place_ref[0] * 128, 128), 128)
    turned = (((0,), (0,)), ((), ()))
    one, two, three = (b[...].astype(F32) for b in back)
    cross = (own[...] + one) + (two + three)
    exact = dict(precision=lax.Precision.HIGHEST, preferred_element_type=F32)
    mixed_far_ref[...] = jnp.dot(cross, cov_ref[:, far_columns], **exact).astype(BF16)
    mixed_ref[...] = jnp.dot(cross, cov_ref[:, own_columns], **exact)
    high = cross.astype(BF16)
    rest = (cross - high.astype(F32)).astype(BF16)
    for columns, cot in ((own_columns, near[...]), (far_columns, far[...])):
        held[:, columns] = lax.dot_general(
            high, cot, turned, preferred_element_type=F32
        ) + lax.dot_general(rest, cot, turned, preferred_element_type=F32)
    core = place_ref[1]
    grad_ref[...] = held[pl.ds(pl.multiple_of(core * 64, 64), 64), :]
    grad_far_ref[...] = held[pl.ds(pl.multiple_of(64 - core * 64, 64), 64), :]


def local(slab_points, key_points, length_weights, adjoint, label_cov, cotangent):
    core, lab = lax.axis_index("pts") & 1, lax.axis_index("lab")

    keys = key_points.astype(F32)
    scaled = (keys * length_weights * (1.0 / 32.0)).astype(BF16)
    key_term = jnp.sum(keys * keys * length_weights, axis=1) * (-1.0 / 64.0)
    high = lax.reduce_precision(key_term, 8, 7)
    rest = key_term - high
    middle = lax.reduce_precision(rest, 8, 7)
    both = jnp.concatenate([scaled, adjoint], axis=1)
    halves = []
    for h in (slice(0, HALF), slice(HALF, 2 * HALF)):
        blank = jnp.zeros((2, 256), F32)
        parts = [jnp.concatenate([t[h].reshape(2, 256), blank]) for t in (high, middle, rest - middle)]
        parts = jnp.concatenate([*parts, blank, blank]).astype(BF16)
        halves += [both[h], parts]
    pack = jnp.concatenate(halves, axis=0)

    right = swap_ring(pack, X, 1)
    left = swap_ring(pack, X, 3)
    own_far = swap(pack, CORE, 1)

    own = in_vmem(gate_kernel, jax.ShapeDtypeStruct((64, 128), BF16), [slab_points, own_far])
    part = jnp.concatenate([own] + [swap(own, Z, m) for m in (1, 2, 3)] + [cotangent], axis=0)
    rows, term, cot, zeros = prepare(
        length_weights, [part] + [swap(part, Y, m) for m in (1, 2, 3)]
    )

    right, left = right + zeros[0:1], left + zeros[0:1]
    upper = swap_ring(right[:528], X, 1)
    lower = swap_ring(left[528:], X, 3)
    right_far, left_far = swap(right, CORE, 1), swap(left, CORE, 1)
    cot_far = swap_lab(cot)

    total, zeros = cross_first(rows, term, None, [pack, own_far, right, right_far])
    upper, lower = upper + zeros[0:1], lower + zeros[0:1]
    upper_far, lower_far = swap(upper, CORE, 1), swap(lower, CORE, 1)
    total, _ = cross_first(rows, term, total, [left, left_far])
    packs = [upper, lower, upper_far, lower_far]
    sent = {
        m: cross_last(m, rows, term, total, packs, F32 if m == 0 else BF16)
        for m in (2, 1, 3, 0)
    }
    back = [swap(sent[m], Z, m) for m in (1, 2, 3)]

    mixed, mixed_far, grad, grad_far = in_vmem(
        grad_kernel,
        (
            jax.ShapeDtypeStruct((256, 128), F32),
            jax.ShapeDtypeStruct((256, 128), BF16),
            jax.ShapeDtypeStruct((64, 256), F32),
            jax.ShapeDtypeStruct((64, 256), F32),
        ),
        [jnp.stack([lab, core]), sent[0], *back, cot, cot_far, label_cov],
        small=0,
        scratch=[pltpu.VMEM((128, 256), F32)],
    )
    mixed = mixed + swap_lab(mixed_far).astype(F32)
    grad = grad + swap(grad_far, CORE, 1)
    back = [swap(grad, X, m) for m in (1, 2, 3)]
    grad = ((grad + back[0]) + (back[1] + back[2])).astype(BF16)

    back = [
        swap(
            jnp.concatenate([mixed[64 * m : 64 * m + 64].astype(BF16), grad], axis=1), Y, m
        ).astype(F32)
        for m in (1, 2, 3)
    ]
    mixed = (mixed[:64] + back[0][:, :128]) + (back[1][:, :128] + back[2][:, :128])
    back = [b[:, 128:] for b in back]
    grad = ((grad.astype(F32) + back[0]) + (back[1] + back[2])).astype(BF16)

    back = [swap(grad, Z, m).astype(F32) for m in (1, 2, 3)]
    grad = (grad.astype(F32) + back[0]) + (back[1] + back[2])
    other = swap(grad, CORE, 1)
    grad = jnp.where(
        core == 0,
        jnp.concatenate([grad, other], axis=0),
        jnp.concatenate([other, grad], axis=0),
    )
    return mixed.astype(BF16), grad


def solution(mesh):
    placed = (P("pts", None), P("pts", None), P(), P("pts", "lab"), P("lab", None), P("pts", "lab"))
    return jax.shard_map(
        local,
        mesh=mesh,
        in_specs=placed,
        out_specs=(P("pts", "lab"), P("lab", None)),
        check_vma=False,
    )
```

```python
import functools

import jax
import jax.numpy as jnp
from jax import lax
from jax.experimental import pallas as pl
from jax.experimental.pallas import tpu as pltpu
from jax.sharding import PartitionSpec as P

F32 = jnp.float32
BF16 = jnp.bfloat16
PTS = 128
HALF = 512
TILE = 256
CORE, X, Z, Y = 0, 1, 3, 5


def swap(value, place, mask):
    return lax.ppermute(value, "pts", [(i, i ^ (mask << place)) for i in range(PTS)])


def swap_ring(value, place, step):
    pairs = []
    for i in range(PTS):
        at = (i >> place) & 3
        pairs.append((i, i + ((((at - step) & 3) - at) << place)))
    return lax.ppermute(value, "pts", pairs)


def swap_lab(value):
    return lax.ppermute(value, "lab", [(0, 1), (1, 0)])


def accumulate(total, rows, row_term, pack):
    for base in range(0, pack.shape[0], HALF + 16):
        terms = pack[base + HALF : base + HALF + 16, :].astype(F32)
        for j in range(HALF // TILE):
            key_term = terms[j : j + 1] + terms[4 + j : 5 + j] + terms[8 + j : 9 + j]
            tile = pl.ds(base + j * TILE, TILE)
            inner = lax.dot_general(
                rows, pack[tile, 0:128], (((1,), (1,)), ((), ())), preferred_element_type=F32
            )
            kernel = jnp.exp(inner + row_term + key_term).astype(BF16)
            total += jnp.dot(kernel, pack[tile, 128:256], preferred_element_type=F32)
    return total


def prepare_kernel(weights_ref, *refs):
    part_refs, (rows_ref, term_ref, cot_ref, zero_ref) = refs[:4], refs[4:]
    weights = weights_ref[...].reshape(1, 128) * (-1.0 / 64.0)
    for d, ref in enumerate(part_refs):
        for m in range(4):
            place = pl.ds(256 * m + 64 * d, 64)
            part = ref[64 * m : 64 * m + 64, :]
            wide = part.astype(F32)
            rows_ref[place, :] = part
            term = jnp.sum(wide * wide * weights, axis=1, keepdims=True)
            term_ref[place, :] = jnp.broadcast_to(term, (64, 128))
        cot_ref[64 * d : 64 * d + 64, :] = ref[256:320, :]
    zero_ref[...] = jnp.zeros_like(zero_ref)


def first_kernel(rows_ref, term_ref, *refs):
    packs, out, zero_ref = refs[:-2], refs[-2], refs[-1]
    for place in (slice(0, 512), slice(512, 1024)):
        total = jnp.zeros((512, 128), F32)
        for pack in packs:
            total = accumulate(total, rows_ref[place, :], term_ref[place, 0:1], pack)
        out[place, :] = total
    zero_ref[...] = jnp.zeros_like(zero_ref)


def last_kernel(first, rows_ref, term_ref, start, *refs):
    packs, outs = refs[-8:-2], refs[-2:]
    place = slice(256 * first, 256 * first + 512)
    total = start[place, :]
    for pack in packs:
        total = accumulate(total, rows_ref[place, :], term_ref[place, 0:1], pack)
    for m, out in enumerate(outs):
        out[...] = total[256 * m : 256 * m + 256].astype(out.dtype)


def in_vmem(kernel, out, args, scratch=()):
    return pl.pallas_call(
        kernel,
        out_shape=out,
        in_specs=[pl.BlockSpec(memory_space=pltpu.VMEM)] * len(args),
        scratch_shapes=scratch,
        out_specs=jax.tree.map(lambda _: pl.BlockSpec(memory_space=pltpu.VMEM), out),
        compiler_params=pltpu.CompilerParams(vmem_limit_bytes=8 * 2**20),
        cost_estimate=pl.CostEstimate(
            flops=1000,
            bytes_accessed=2 * 2**20,
            transcendentals=0,
        ),
    )(*args)


ZEROS = jax.ShapeDtypeStruct((16, 256), BF16)


def prepare(weights, rows):
    return in_vmem(
        prepare_kernel,
        (
            jax.ShapeDtypeStruct((1024, 128), BF16),
            jax.ShapeDtypeStruct((1024, 128), F32),
            jax.ShapeDtypeStruct((256, 128), BF16),
            ZEROS,
        ),
        [weights, *rows],
    )


def cross_first(rows, term, packs):
    return in_vmem(
        first_kernel, (jax.ShapeDtypeStruct((1024, 128), F32), ZEROS), [rows, term, *packs]
    )


def cross_last(first, rows, term, total, packs, earlier=()):
    outs = [jax.ShapeDtypeStruct((256, 128), BF16 if m else F32) for m in (first, first + 1)]
    args = [rows, term, total, *earlier, *packs]
    return in_vmem(functools.partial(last_kernel, first), outs, args)


def gate_kernel(value_ref, _, out_ref):
    out_ref[...] = value_ref[...]


def halves_kernel(right_ref, left_ref, *refs):
    upper_ref, lower_ref, zero_ref = refs[-3:]
    zero_ref[...] = jnp.zeros_like(zero_ref)
    upper_ref[...] = right_ref[0:528, :]
    lower_ref[...] = left_ref[528:1056, :]


def grad_kernel(own, *refs):
    back, near, far, cov_ref = refs[:3], refs[3], refs[4], refs[5]
    mixed_ref, mixed_far_ref, grad_ref, grad_far_ref, held = refs[6:]
    lab, core = lax.axis_index("lab"), lax.axis_index("pts") & 1
    own_columns = pl.ds(pl.multiple_of(lab * 128, 128), 128)
    far_columns = pl.ds(pl.multiple_of(128 - lab * 128, 128), 128)
    turned = (((0,), (0,)), ((), ()))
    one, two, three = (b[...].astype(F32) for b in back)
    cross = (own[...] + one) + (two + three)
    exact = dict(precision=lax.Precision.HIGHEST, preferred_element_type=F32)
    mixed_far_ref[...] = jnp.dot(cross, cov_ref[:, far_columns], **exact).astype(BF16)
    mixed_ref[...] = jnp.dot(cross, cov_ref[:, own_columns], **exact)
    high = cross.astype(BF16)
    rest = (cross - high.astype(F32)).astype(BF16)
    for columns, cot in ((own_columns, near[...]), (far_columns, far[...])):
        held[:, columns] = lax.dot_general(
            high, cot, turned, preferred_element_type=F32
        ) + lax.dot_general(rest, cot, turned, preferred_element_type=F32)
    grad_ref[...] = held[pl.ds(pl.multiple_of(core * 64, 64), 64), :]
    grad_far_ref[...] = held[pl.ds(pl.multiple_of(64 - core * 64, 64), 64), :]


def join_kernel(own_ref, other_ref, out_ref):
    core = lax.axis_index("pts") & 1
    out_ref[pl.ds(pl.multiple_of(core * 64, 64), 64), :] = own_ref[...]
    out_ref[pl.ds(pl.multiple_of(64 - core * 64, 64), 64), :] = other_ref[...]


def local(slab_points, key_points, length_weights, adjoint, label_cov, cotangent):

    keys = key_points.astype(F32)
    scaled = (keys * length_weights * (1.0 / 32.0)).astype(BF16)
    key_term = jnp.sum(keys * keys * length_weights, axis=1) * (-1.0 / 64.0)
    high = lax.reduce_precision(key_term, 8, 7)
    rest = key_term - high
    middle = lax.reduce_precision(rest, 8, 7)
    both = jnp.concatenate([scaled, adjoint], axis=1)
    halves = []
    for h in (slice(0, HALF), slice(HALF, 2 * HALF)):
        blank = jnp.zeros((2, 256), F32)
        parts = [jnp.concatenate([t[h].reshape(2, 256), blank]) for t in (high, middle, rest - middle)]
        parts = jnp.concatenate([*parts, blank, blank]).astype(BF16)
        halves += [both[h], parts]
    pack = jnp.concatenate(halves, axis=0)

    right, left = swap_ring(pack, X, 1), swap_ring(pack, X, 3)
    own_far = swap(pack, CORE, 1)

    own = in_vmem(gate_kernel, jax.ShapeDtypeStruct((64, 128), BF16), [slab_points, own_far])
    part = jnp.concatenate([own] + [swap(own, Z, m) for m in (1, 2, 3)] + [cotangent], axis=0)
    parts = [part] + [swap(part, Y, m) for m in (1, 2, 3)]
    rows, term, cot, _ = prepare(length_weights, parts)

    half = jax.ShapeDtypeStruct((528, 256), BF16)
    upper, lower, zeros = in_vmem(halves_kernel, (half, half, ZEROS), [right, left, parts[1]])
    upper, lower = swap_ring(upper, X, 1), swap_ring(lower, X, 3)
    right_far, left_far = swap(right + zeros[0:1], CORE, 1), swap(left + zeros[0:1], CORE, 1)

    total, zeros = cross_first(rows, term, [pack, own_far, right, left])
    upper, lower = upper + zeros[0:1], lower + zeros[0:1]
    cot_far = swap_lab(cot)
    packs = [right_far, left_far, upper, lower, swap(upper, CORE, 1), swap(lower, CORE, 1)]
    sent = cross_last(2, rows, term, total, packs)
    sent = cross_last(0, rows, term, total, packs, sent[:1]) + sent
    back = [swap(sent[m], Z, m) for m in (1, 2, 3)]

    mixed, mixed_far, grad, grad_far = in_vmem(
        grad_kernel,
        (
            jax.ShapeDtypeStruct((256, 128), F32),
            jax.ShapeDtypeStruct((256, 128), BF16),
            jax.ShapeDtypeStruct((64, 256), F32),
            jax.ShapeDtypeStruct((64, 256), F32),
        ),
        [sent[0], *back, cot, cot_far, label_cov],
        scratch=[pltpu.VMEM((128, 256), F32)],
    )
    mixed = mixed + swap_lab(mixed_far).astype(F32)
    grad = grad + swap(grad_far, CORE, 1)
    back = [swap(grad, X, m) for m in (1, 2, 3)]
    grad = ((grad + back[0]) + (back[1] + back[2])).astype(BF16)

    back = [swap(grad, Z, m).astype(F32) for m in (1, 2, 3)]
    grad = ((grad.astype(F32) + back[0]) + (back[1] + back[2])).astype(BF16)

    back = [
        swap(
            jnp.concatenate([mixed[64 * m : 64 * m + 64].astype(BF16), grad], axis=1), Y, m
        ).astype(F32)
        for m in (1, 2, 3)
    ]
    mixed = (mixed[:64] + back[0][:, :128]) + (back[1][:, :128] + back[2][:, :128])
    back = [b[:, 128:] for b in back]
    grad = (grad.astype(F32) + back[0]) + (back[1] + back[2])
    grad = in_vmem(
        join_kernel, jax.ShapeDtypeStruct((128, 256), F32), [grad, swap(grad, CORE, 1)]
    )
    return mixed.astype(BF16), grad


def solution(mesh):
    placed = (P("pts", None), P("pts", None), P(), P("pts", "lab"), P("lab", None), P("pts", "lab"))
    return jax.shard_map(
        local,
        mesh=mesh,
        in_specs=placed,
        out_specs=(P("pts", "lab"), P("lab", None)),
        check_vma=False,
    )
```

```python
import functools

import jax
import jax.numpy as jnp
from jax import lax
from jax.experimental import pallas as pl
from jax.experimental.pallas import tpu as pltpu
from jax.sharding import PartitionSpec as P

F32 = jnp.float32
BF16 = jnp.bfloat16
PTS = 128
HALF = 512
TILE = 256
CORE, X, Z, Y = 0, 1, 3, 5


def swap(value, place, mask):
    return lax.ppermute(value, "pts", [(i, i ^ (mask << place)) for i in range(PTS)])


def swap_ring(value, place, step):
    pairs = []
    for i in range(PTS):
        at = (i >> place) & 3
        pairs.append((i, i + ((((at - step) & 3) - at) << place)))
    return lax.ppermute(value, "pts", pairs)


def swap_lab(value):
    return lax.ppermute(value, "lab", [(0, 1), (1, 0)])


def accumulate(total, rows, row_term, pack):
    for base in range(0, pack.shape[0], HALF + 16):
        terms = pack[base + HALF : base + HALF + 16, :].astype(F32)
        for j in range(HALF // TILE):
            key_term = terms[j : j + 1] + terms[4 + j : 5 + j] + terms[8 + j : 9 + j]
            tile = pl.ds(base + j * TILE, TILE)
            inner = lax.dot_general(
                rows, pack[tile, 0:128], (((1,), (1,)), ((), ())), preferred_element_type=F32
            )
            kernel = jnp.exp(inner + row_term + key_term).astype(BF16)
            total += jnp.dot(kernel, pack[tile, 128:256], preferred_element_type=F32)
    return total


def prepare_kernel(weights_ref, *refs):
    part_refs, (rows_ref, term_ref) = refs[:4], refs[4:]
    weights = weights_ref[...].reshape(1, 128) * (-1.0 / 64.0)
    for d, ref in enumerate(part_refs):
        place = slice(256 * d, 256 * d + 256)
        part = ref[...]
        wide = part.astype(F32)
        rows_ref[place, :] = part
        term = jnp.sum(wide * wide * weights, axis=1, keepdims=True)
        term_ref[place, :] = jnp.broadcast_to(term, (256, 128))


def first_kernel(rows_ref, term_ref, *refs):
    packs, out, zero_ref = refs[:-2], refs[-2], refs[-1]
    for place in (slice(0, 512), slice(512, 1024)):
        total = jnp.zeros((512, 128), F32)
        for pack in packs:
            total = accumulate(total, rows_ref[place, :], term_ref[place, 0:1], pack)
        out[place, :] = total
    zero_ref[...] = jnp.zeros_like(zero_ref)


def last_kernel(blocks, rows_ref, term_ref, start, *refs):
    packs, outs = refs[-6 - len(blocks) : -len(blocks)], refs[-len(blocks) :]
    place = slice(256 * blocks[0], 256 * blocks[-1] + 256)
    total = start[place, :]
    for pack in packs:
        total = accumulate(total, rows_ref[place, :], term_ref[place, 0:1], pack)
    for m, out in enumerate(outs):
        out[...] = total[256 * m : 256 * m + 256].astype(out.dtype)


def in_vmem(kernel, out, args, scratch=()):
    return pl.pallas_call(
        kernel,
        out_shape=out,
        in_specs=[pl.BlockSpec(memory_space=pltpu.VMEM)] * len(args),
        scratch_shapes=scratch,
        out_specs=jax.tree.map(lambda _: pl.BlockSpec(memory_space=pltpu.VMEM), out),
        compiler_params=pltpu.CompilerParams(vmem_limit_bytes=8 * 2**20),
        cost_estimate=pl.CostEstimate(
            flops=1000,
            bytes_accessed=2 * 2**20,
            transcendentals=0,
        ),
    )(*args)


ZEROS = jax.ShapeDtypeStruct((16, 256), BF16)


def prepare(weights, parts):
    return in_vmem(
        prepare_kernel,
        (jax.ShapeDtypeStruct((1024, 128), BF16), jax.ShapeDtypeStruct((1024, 128), F32)),
        [weights, *parts],
    )


def cross_first(rows, term, packs):
    return in_vmem(
        first_kernel, (jax.ShapeDtypeStruct((1024, 128), F32), ZEROS), [rows, term, *packs]
    )


def cross_last(blocks, rows, term, total, packs, earlier=()):
    outs = [jax.ShapeDtypeStruct((256, 128), BF16 if m else F32) for m in blocks]
    args = [rows, term, total, *earlier, *packs]
    return in_vmem(functools.partial(last_kernel, blocks), outs, args)


def gate_kernel(slab_ref, cotangent_ref, _, out_ref):
    out_ref[0:64, :] = slab_ref[...]
    out_ref[64:128, :] = cotangent_ref[...]


def halves_kernel(right_ref, left_ref, *refs):
    upper_ref, lower_ref, zero_ref = refs[-3:]
    zero_ref[...] = jnp.zeros_like(zero_ref)
    upper_ref[...] = right_ref[0:528, :]
    lower_ref[...] = left_ref[528:1056, :]


def grad_kernel(own, *refs):
    back, near, far, cov_ref = refs[:3], refs[3], refs[4], refs[5]
    mixed_ref, mixed_far_ref, grad_ref, grad_far_ref, held = refs[6:]
    lab, core = lax.axis_index("lab"), lax.axis_index("pts") & 1
    own_columns = pl.ds(pl.multiple_of(lab * 128, 128), 128)
    far_columns = pl.ds(pl.multiple_of(128 - lab * 128, 128), 128)
    turned = (((0,), (0,)), ((), ()))
    one, two, three = (b[...].astype(F32) for b in back)
    cross = (own[...] + one) + (two + three)
    exact = dict(precision=lax.Precision.HIGHEST, preferred_element_type=F32)
    mixed_far_ref[...] = jnp.dot(cross, cov_ref[:, far_columns], **exact).astype(BF16)
    mixed_ref[...] = jnp.dot(cross, cov_ref[:, own_columns], **exact)
    high = cross.astype(BF16)
    rest = (cross - high.astype(F32)).astype(BF16)
    for columns, cot in ((own_columns, near[...]), (far_columns, far[...])):
        held[:, columns] = lax.dot_general(
            high, cot, turned, preferred_element_type=F32
        ) + lax.dot_general(rest, cot, turned, preferred_element_type=F32)
    grad_ref[...] = held[pl.ds(pl.multiple_of(core * 64, 64), 64), :]
    grad_far_ref[...] = held[pl.ds(pl.multiple_of(64 - core * 64, 64), 64), :]


def join_kernel(own_ref, other_ref, out_ref):
    core = lax.axis_index("pts") & 1
    out_ref[pl.ds(pl.multiple_of(core * 64, 64), 64), :] = own_ref[...]
    out_ref[pl.ds(pl.multiple_of(64 - core * 64, 64), 64), :] = other_ref[...]


def local(slab_points, key_points, length_weights, adjoint, label_cov, cotangent):
    keys = key_points.astype(F32)
    scaled = (keys * length_weights * (1.0 / 32.0)).astype(BF16)
    key_term = jnp.sum(keys * keys * length_weights, axis=1) * (-1.0 / 64.0)
    high = lax.reduce_precision(key_term, 8, 7)
    rest = key_term - high
    middle = lax.reduce_precision(rest, 8, 7)
    both = jnp.concatenate([scaled, adjoint], axis=1)
    halves = []
    for h in (slice(0, HALF), slice(HALF, 2 * HALF)):
        blank = jnp.zeros((2, 256), F32)
        parts = [jnp.concatenate([t[h].reshape(2, 256), blank]) for t in (high, middle, rest - middle)]
        parts = jnp.concatenate([*parts, blank, blank]).astype(BF16)
        halves += [both[h], parts]
    pack = jnp.concatenate(halves, axis=0)

    right, left = swap_ring(pack, X, 1), swap_ring(pack, X, 3)
    own_far = swap(pack, CORE, 1)

    own = jax.ShapeDtypeStruct((128, 128), BF16)
    own = in_vmem(gate_kernel, own, [slab_points, cotangent, own_far])
    over_z = [own] + [swap(own, Z, m) for m in (1, 2, 3)]
    part = jnp.concatenate([o[:64] for o in over_z], axis=0)
    cot = jnp.concatenate([o[64:] for o in over_z], axis=0)
    parts = [part] + [swap(part, Y, m) for m in (1, 2, 3)]
    rows, term = prepare(length_weights, parts)

    half = jax.ShapeDtypeStruct((528, 256), BF16)
    upper, lower, zeros = in_vmem(halves_kernel, (half, half, ZEROS), [right, left, parts[1]])
    upper, lower = swap_ring(upper, X, 1), swap_ring(lower, X, 3)
    right_far, left_far = swap(right + zeros[0:1], CORE, 1), swap(left + zeros[0:1], CORE, 1)

    total, zeros = cross_first(rows, term, [pack, own_far, right, left])
    upper, lower = upper + zeros[0:1], lower + zeros[0:1]
    cot_far = swap_lab(cot)
    packs = [right_far, left_far, upper, lower, swap(upper, CORE, 1), swap(lower, CORE, 1)]
    sent = cross_last((1, 2, 3), rows, term, total, packs)
    sent = cross_last((0,), rows, term, total, packs, sent[:1]) + sent
    back = [swap(sent[m], Y, m) for m in (1, 2, 3)]

    mixed, mixed_far, grad, grad_far = in_vmem(
        grad_kernel,
        (
            jax.ShapeDtypeStruct((256, 128), F32),
            jax.ShapeDtypeStruct((256, 128), BF16),
            jax.ShapeDtypeStruct((64, 256), F32),
            jax.ShapeDtypeStruct((64, 256), F32),
        ),
        [sent[0], *back, cot, cot_far, label_cov],
        scratch=[pltpu.VMEM((128, 256), F32)],
    )
    mixed = mixed + swap_lab(mixed_far).astype(F32)
    grad = grad + swap(grad_far, CORE, 1)
    back = [swap(grad, X, m) for m in (1, 2, 3)]
    grad = ((grad + back[0]) + (back[1] + back[2])).astype(BF16)

    back = [swap(grad, Y, m).astype(F32) for m in (1, 2, 3)]
    grad = ((grad.astype(F32) + back[0]) + (back[1] + back[2])).astype(BF16)

    back = [
        swap(
            jnp.concatenate([mixed[64 * m : 64 * m + 64].astype(BF16), grad], axis=1), Z, m
        ).astype(F32)
        for m in (1, 2, 3)
    ]
    mixed = (mixed[:64] + back[0][:, :128]) + (back[1][:, :128] + back[2][:, :128])
    back = [b[:, 128:] for b in back]
    grad = (grad.astype(F32) + back[0]) + (back[1] + back[2])
    grad = in_vmem(
        join_kernel, jax.ShapeDtypeStruct((128, 256), F32), [grad, swap(grad, CORE, 1)]
    )
    return mixed.astype(BF16), grad


def solution(mesh):
    placed = (P("pts", None), P("pts", None), P(), P("pts", "lab"), P("lab", None), P("pts", "lab"))
    return jax.shard_map(
        local,
        mesh=mesh,
        in_specs=placed,
        out_specs=(P("pts", "lab"), P("lab", None)),
        check_vma=False,
    )
```

```python
import functools

import jax
import jax.numpy as jnp
from jax import lax
from jax.experimental import pallas as pl
from jax.experimental.pallas import tpu as pltpu
from jax.sharding import PartitionSpec as P

F32 = jnp.float32
BF16 = jnp.bfloat16
PTS = 128
HALF = 512
TILE = 256
CORE, X, Z, Y = 0, 1, 3, 5


def swap(value, place, mask):
    return lax.ppermute(value, "pts", [(i, i ^ (mask << place)) for i in range(PTS)])


def swap_ring(value, place, step):
    pairs = []
    for i in range(PTS):
        at = (i >> place) & 3
        pairs.append((i, i + ((((at - step) & 3) - at) << place)))
    return lax.ppermute(value, "pts", pairs)


def swap_lab(value):
    return lax.ppermute(value, "lab", [(0, 1), (1, 0)])


def accumulate(total, rows, row_term, pack):
    for base in range(0, pack.shape[0], HALF + 16):
        terms = pack[base + HALF : base + HALF + 16, :].astype(F32)
        for j in range(HALF // TILE):
            key_term = terms[j : j + 1] + terms[4 + j : 5 + j] + terms[8 + j : 9 + j]
            tile = pl.ds(base + j * TILE, TILE)
            inner = lax.dot_general(
                rows, pack[tile, 0:128], (((1,), (1,)), ((), ())), preferred_element_type=F32
            )
            kernel = jnp.exp(inner + row_term + key_term).astype(BF16)
            total += jnp.dot(kernel, pack[tile, 128:256], preferred_element_type=F32)
    return total


def prepare_kernel(weights_ref, *refs):
    part_refs, (rows_ref, term_ref) = refs[:4], refs[4:]
    weights = weights_ref[...].reshape(1, 128) * (-1.0 / 64.0)
    for d, ref in enumerate(part_refs):
        place = slice(256 * d, 256 * d + 256)
        part = ref[...]
        wide = part.astype(F32)
        rows_ref[place, :] = part
        term = jnp.sum(wide * wide * weights, axis=1, keepdims=True)
        term_ref[place, :] = jnp.broadcast_to(term, (256, 128))


def first_kernel(rows_ref, term_ref, *refs):
    packs, out, zero_ref = refs[:-2], refs[-2], refs[-1]
    for place in (slice(0, 512), slice(512, 1024)):
        total = jnp.zeros((512, 128), F32)
        for pack in packs:
            total = accumulate(total, rows_ref[place, :], term_ref[place, 0:1], pack)
        out[place, :] = total
    zero_ref[...] = jnp.zeros_like(zero_ref)


def last_kernel(blocks, rows_ref, term_ref, start, *refs):
    packs, outs = refs[-6 - len(blocks) : -len(blocks)], refs[-len(blocks) :]
    place = slice(256 * blocks[0], 256 * blocks[-1] + 256)
    total = start[place, :]
    for pack in packs:
        total = accumulate(total, rows_ref[place, :], term_ref[place, 0:1], pack)
    for m, out in enumerate(outs):
        out[...] = total[256 * m : 256 * m + 256].astype(out.dtype)


def in_vmem(kernel, out, args, scratch=()):
    return pl.pallas_call(
        kernel,
        out_shape=out,
        in_specs=[pl.BlockSpec(memory_space=pltpu.VMEM)] * len(args),
        scratch_shapes=scratch,
        out_specs=jax.tree.map(lambda _: pl.BlockSpec(memory_space=pltpu.VMEM), out),
        compiler_params=pltpu.CompilerParams(vmem_limit_bytes=8 * 2**20),
        cost_estimate=pl.CostEstimate(
            flops=1000,
            bytes_accessed=2 * 2**20,
            transcendentals=0,
        ),
    )(*args)


ZEROS = jax.ShapeDtypeStruct((16, 256), BF16)


def prepare(weights, parts):
    return in_vmem(
        prepare_kernel,
        (jax.ShapeDtypeStruct((1024, 128), BF16), jax.ShapeDtypeStruct((1024, 128), F32)),
        [weights, *parts],
    )


def cross_first(rows, term, packs):
    return in_vmem(
        first_kernel, (jax.ShapeDtypeStruct((1024, 128), F32), ZEROS), [rows, term, *packs]
    )


def cross_last(blocks, rows, term, total, packs, earlier=()):
    outs = [jax.ShapeDtypeStruct((256, 128), BF16 if m else F32) for m in blocks]
    args = [rows, term, total, *earlier, *packs]
    return in_vmem(functools.partial(last_kernel, blocks), outs, args)


def gate_kernel(slab_ref, cotangent_ref, _, out_ref):
    out_ref[0:64, :] = slab_ref[...]
    out_ref[64:128, :] = cotangent_ref[...]


def halves_kernel(right_ref, left_ref, *refs):
    upper_ref, lower_ref, zero_ref = refs[-3:]
    zero_ref[...] = jnp.zeros_like(zero_ref)
    upper_ref[...] = right_ref[0:528, :]
    lower_ref[...] = left_ref[528:1056, :]


def grad_kernel(own, *refs):
    back, near, far, cov_ref = refs[:3], refs[3], refs[4], refs[5]
    mixed_ref, mixed_far_ref, grad_ref, grad_far_ref, held = refs[6:]
    lab, core = lax.axis_index("lab"), lax.axis_index("pts") & 1
    own_columns = pl.ds(pl.multiple_of(lab * 128, 128), 128)
    far_columns = pl.ds(pl.multiple_of(128 - lab * 128, 128), 128)
    turned = (((0,), (0,)), ((), ()))
    one, two, three = (b[...].astype(F32) for b in back)
    cross = (own[...] + one) + (two + three)
    exact = dict(precision=lax.Precision.HIGHEST, preferred_element_type=F32)
    mixed_far_ref[...] = jnp.dot(cross, cov_ref[:, far_columns], **exact).astype(BF16)
    mixed_ref[...] = jnp.dot(cross, cov_ref[:, own_columns], **exact)
    high = cross.astype(BF16)
    rest = (cross - high.astype(F32)).astype(BF16)
    for columns, cot in ((own_columns, near[...]), (far_columns, far[...])):
        held[:, columns] = lax.dot_general(
            high, cot, turned, preferred_element_type=F32
        ) + lax.dot_general(rest, cot, turned, preferred_element_type=F32)
    grad_ref[...] = held[pl.ds(pl.multiple_of(core * 64, 64), 64), :]
    grad_far_ref[...] = held[pl.ds(pl.multiple_of(64 - core * 64, 64), 64), :]


def join_kernel(own_ref, other_ref, mixed_ref, mixed_out_ref, out_ref):
    mixed_out_ref[...] = mixed_ref[...].astype(BF16)
    core = lax.axis_index("pts") & 1
    out_ref[pl.ds(pl.multiple_of(core * 64, 64), 64), :] = own_ref[...]
    out_ref[pl.ds(pl.multiple_of(64 - core * 64, 64), 64), :] = other_ref[...]


def local(slab_points, key_points, length_weights, adjoint, label_cov, cotangent):
    keys = key_points.astype(F32)
    scaled = (keys * length_weights * (1.0 / 32.0)).astype(BF16)
    key_term = jnp.sum(keys * keys * length_weights, axis=1) * (-1.0 / 64.0)
    high = lax.reduce_precision(key_term, 8, 7)
    rest = key_term - high
    middle = lax.reduce_precision(rest, 8, 7)
    both = jnp.concatenate([scaled, adjoint], axis=1)
    halves = []
    for h in (slice(0, HALF), slice(HALF, 2 * HALF)):
        blank = jnp.zeros((2, 256), F32)
        parts = [jnp.concatenate([t[h].reshape(2, 256), blank]) for t in (high, middle, rest - middle)]
        parts = jnp.concatenate([*parts, blank, blank]).astype(BF16)
        halves += [both[h], parts]
    pack = jnp.concatenate(halves, axis=0)

    right, left = swap_ring(pack, X, 1), swap_ring(pack, X, 3)
    own_far = swap(pack, CORE, 1)

    own = jax.ShapeDtypeStruct((128, 128), BF16)
    own = in_vmem(gate_kernel, own, [slab_points, cotangent, own_far])
    over_z = [own] + [swap(own, Z, m) for m in (1, 2, 3)]
    part = jnp.concatenate([o[:64] for o in over_z], axis=0)
    cot = jnp.concatenate([o[64:] for o in over_z], axis=0)
    parts = [part] + [swap(part, Y, m) for m in (1, 2, 3)]
    rows, term = prepare(length_weights, parts)

    half = jax.ShapeDtypeStruct((528, 256), BF16)
    upper, lower, zeros = in_vmem(halves_kernel, (half, half, ZEROS), [right, left, parts[1]])
    upper, lower = swap_ring(upper, X, 1), swap_ring(lower, X, 3)
    right_far, left_far = swap(right + zeros[0:1], CORE, 1), swap(left + zeros[0:1], CORE, 1)

    total, zeros = cross_first(rows, term, [pack, own_far, right, left])
    upper, lower = upper + zeros[0:1], lower + zeros[0:1]
    cot_far = swap_lab(cot)
    packs = [right_far, left_far, upper, lower, swap(upper, CORE, 1), swap(lower, CORE, 1)]
    sent = cross_last((1, 2, 3), rows, term, total, packs)
    sent = cross_last((0,), rows, term, total, packs, sent[:1]) + sent
    back = [swap(sent[m], Y, m) for m in (1, 2, 3)]

    mixed, mixed_far, grad, grad_far = in_vmem(
        grad_kernel,
        (
            jax.ShapeDtypeStruct((256, 128), F32),
            jax.ShapeDtypeStruct((256, 128), BF16),
            jax.ShapeDtypeStruct((64, 256), F32),
            jax.ShapeDtypeStruct((64, 256), F32),
        ),
        [sent[0], *back, cot, cot_far, label_cov],
        scratch=[pltpu.VMEM((128, 256), F32)],
    )
    mixed = mixed + swap_lab(mixed_far).astype(F32)
    grad = grad + swap(grad_far, CORE, 1)
    back = [swap(grad, X, m) for m in (1, 2, 3)]
    grad = ((grad + back[0]) + (back[1] + back[2])).astype(BF16)

    back = [swap(grad, Y, m).astype(F32) for m in (1, 2, 3)]
    grad = ((grad.astype(F32) + back[0]) + (back[1] + back[2])).astype(BF16)

    back = [
        swap(
            jnp.concatenate([mixed[64 * m : 64 * m + 64].astype(BF16), grad], axis=1), Z, m
        ).astype(F32)
        for m in (1, 2, 3)
    ]
    mixed = (mixed[:64] + back[0][:, :128]) + (back[1][:, :128] + back[2][:, :128])
    back = [b[:, 128:] for b in back]
    grad = (grad.astype(F32) + back[0]) + (back[1] + back[2])
    return in_vmem(
        join_kernel,
        (jax.ShapeDtypeStruct((64, 128), BF16), jax.ShapeDtypeStruct((128, 256), F32)),
        [grad, swap(grad, CORE, 1), mixed],
    )


def solution(mesh):
    placed = (P("pts", None), P("pts", None), P(), P("pts", "lab"), P("lab", None), P("pts", "lab"))
    return jax.shard_map(
        local,
        mesh=mesh,
        in_specs=placed,
        out_specs=(P("pts", "lab"), P("lab", None)),
        check_vma=False,
    )
```
